512 devices in a mesh: ctx: 64 (over z, x), grp: 8 (over y, core).
Axes of the slice: x: 4, y: 4, z: 16, core: 2. Of those that a mesh axis runs over, the one named last changes fastest.
Arguments:
- queries: bfloat16 [8, 16384, 2560], P('grp', 'ctx'), may hold values from -8 to 8
- keys: bfloat16 [8, 16384, 512], P('grp', 'ctx'), may hold values from -6 to 6
- values: bfloat16 [8, 16384, 512], P('grp', 'ctx'), may hold values from -6 to 6
- upstream: bfloat16 [8, 16384, 2560], P('grp', 'ctx'), may hold values from -6 to 6
- lengths: int32 [8, 64], P('grp'), may hold values from 1 to 512, 16384 in all within a row
- group_ids: int32 [8, 64], P('grp'), may hold values from 0 to 31
- rewards: float32 [8, 64], P('grp'), may hold values from -4 to 4
Outputs:
- query_grad: bfloat16 [8, 16384, 2560], P('grp', 'ctx')
- key_grad: bfloat16 [8, 16384, 512], P('grp', 'ctx')
- value_grad: bfloat16 [8, 16384, 512], P('grp', 'ctx')
The draws below stay inside these ranges and needn't reach their ends.
Inputs may be any that keep to these rules, and one draw needn't show every extreme that they name: Each row's lengths sum to 16384; in every row the longest trajectory has exactly 512 positions.
All inputs are finite; a program needn't handle non-finite values.
Results may differ from the reference program's by a relative error of at most 0.02.
Values may be sent and summed in bfloat16 or wider, within the bound.
No kernel may reach another device: no remote copies, remote signals or barrier semaphores. Data moves between devices by JAX's collectives and lax.ppermute only.
A program may use at most 64 MiB of HBM per device.

```python
import math
import jax
import jax.numpy as jnp
import numpy as np
from jax import lax

QH = 20
KVH = 4
HEAD = 128
TOK_DEV = 256
SPAN = 2
TRAJ = 64
ROW = 16384
ROWS = 8
MOST = 512
GROUPS = 32


def shared_table(key):
    normal_part = jax.random.normal(key, (ROWS, ROW, KVH * HEAD), jnp.float32)
    return normal_part


def draw_keys(key, part):
    normal_part = shared_table(key)
    table = jnp.clip(normal_part, -6.0, 6.0)
    return table.astype(jnp.bfloat16)


def draw_queries(key, part):
    key = jax.random.fold_in(key, 22)
    table = jnp.clip(jax.random.normal(key, (ROWS, ROW, QH * HEAD), jnp.float32), -6.0, 6.0)
    return table.astype(jnp.bfloat16)


def place_ends(drawn, own_key, smallest, largest):
    index_at = [jax.random.randint(jax.random.fold_in(own_key, axis), (), 0, length) for axis, length in enumerate(drawn.shape)]
    widest = drawn.shape.index(max(drawn.shape))
    neighbour = index_at[:widest] + [(index_at[widest] + 1) % drawn.shape[widest]] + index_at[widest + 1:]
    return drawn.at[tuple(index_at)].set(smallest).at[tuple(neighbour)].set(largest)


def block_levels(stream_key, dims, shards, low, top_value):
    def one(axis_at, parts):
        steps = jax.random.uniform(jax.random.fold_in(jax.random.fold_in(stream_key, 6), axis_at), (parts,), jnp.float32, low / len(shards), top_value / len(shards))
        return jnp.repeat(jnp.exp(steps), dims[axis_at] // parts).reshape((-1,) + (1,) * (len(dims) - axis_at - 1))

    gain = one(*shards[0])
    for cut in shards[1:]:
        gain = gain * one(*cut)
    return gain


def split_up(amount, total, bound, slope):
    portions = [(1 << 20) // math.isqrt(standing ** slope) + 1 for standing in range(2, amount + 1)]
    spare, given = total - bound - (amount - 1), [1] * (amount - 1)
    while spare > 0:
        candidates = [i for i in range(amount - 1) if given[i] < bound]
        pool, left = sum([portions[i] for i in candidates]), spare
        for i in candidates:
            addition = min(bound - given[i], max(1, left * portions[i] // pool), spare)
            given[i] = given[i] + addition
            spare = spare - addition
    return np.array([bound] + given)


def uneven_parts(own_key, amount, total, bound, skew):
    if amount == 2:
        one = jax.random.randint(own_key, (), max(1, total - bound), min(bound, total - 1) + 1)
        return jnp.stack([one, total - one])
    sizes = jnp.asarray(split_up(amount, total, bound, skew), jnp.int32)
    pairs = (amount - 1) // 2
    donor, taker = sizes[1:1 + 2 * pairs:2], sizes[2:2 + 2 * pairs:2]
    slack = jnp.minimum(donor - 1, bound - taker)
    moved = jax.random.randint(jax.random.fold_in(own_key, 1), (pairs,), 0, 1 << 20) % (slack + 1)
    sizes = sizes.at[1:1 + 2 * pairs:2].set(donor - moved).at[2:2 + 2 * pairs:2].set(taker + moved)
    return sizes[jax.random.permutation(jax.random.fold_in(own_key, 2), amount)]


def centred(own_key, extent, spread, most, cuts=(), kind=jnp.bfloat16):
    values = jax.random.normal(own_key, extent, jnp.float32) * spread
    if len(cuts) > 0:
        values = block_levels(own_key, extent, cuts, -0.22, 0.18) * values
    return jnp.clip(values, min=-most, max=most).astype(kind)


def setup_inputs(seed: int = 0) -> dict:
    seeds = jax.random.split(jax.random.key(seed), 8)
    return {
        "queries": draw_queries(jax.random.fold_in(seeds[7], 71), 0),
        "keys": draw_keys(jax.random.fold_in(seeds[7], 71), 0),
        "values": centred(seeds[2], (ROWS, ROW, KVH * HEAD), 1.0, 6.0, ((0, 8), (1, 64))),
        "upstream": centred(seeds[3], (ROWS, ROW, QH * HEAD), 1.0, 6.0, ((0, 8), (1, 64))),
        "lengths": jax.vmap(lambda own: uneven_parts(own, TRAJ, ROW, MOST, 1))(jax.random.split(seeds[4], ROWS)).reshape((ROWS, TRAJ)).astype(jnp.int32),
        "group_ids": place_ends(jax.random.randint(seeds[5], (ROWS, TRAJ), 0, GROUPS), jax.random.fold_in(seeds[5], 1), 0, GROUPS - 1).astype(jnp.int32),
        "rewards": centred(seeds[6], (ROWS, TRAJ), 1.0, 4.0, ((0, 8),), jnp.float32),
    }


def segment_of(starts, positions):
    return (lax.optimization_barrier(jnp.sum((positions[:, None] >= starts[None, :]).astype(jnp.int32), axis=1)) - 1).astype(jnp.int32)

def group_backward(query_part, key_part, value_part, weighted_part, allowed):
    score_scale = 1.0 / math.sqrt(HEAD)
    query_f = query_part.astype(jnp.float32)
    key_f = key_part.astype(jnp.float32)
    value_f = value_part.astype(jnp.float32)
    weighted_f = weighted_part.astype(jnp.float32)
    scores = jnp.einsum('tjd,sd->jts', query_f, key_f) * score_scale
    scores = jnp.where(allowed[None], scores, -jnp.inf)
    row_max = lax.optimization_barrier(jnp.max(scores, axis=2, keepdims=True))
    log_total = row_max + jnp.log(lax.optimization_barrier(jnp.sum(jnp.exp(scores - row_max), axis=2, keepdims=True)))
    soft_weights = jnp.exp(scores - log_total).astype(jnp.bfloat16).astype(jnp.float32)
    attended = jnp.einsum('jts,sd->tjd', soft_weights, value_f).astype(jnp.bfloat16)
    delta_sum = lax.optimization_barrier(jnp.sum(weighted_f * attended.astype(jnp.float32), axis=2))
    grad_soft = jnp.einsum('tjd,sd->jts', weighted_f, value_f)
    grad_score = (soft_weights * (grad_soft - jnp.transpose(delta_sum)[:, :, None]) * score_scale).astype(jnp.bfloat16).astype(jnp.float32)
    query_grad = jnp.einsum('jts,sd->tjd', grad_score, key_f).astype(jnp.bfloat16)
    key_grad = jnp.einsum('jts,tjd->sd', grad_score, query_f)
    value_grad = jnp.einsum('jts,tjd->sd', soft_weights, weighted_f)
    return (query_grad, key_grad, value_grad)

def row_backward(row_queries, row_keys, row_values, row_up, row_lengths, row_advantage):
    reach = SPAN * TOK_DEV
    width_kv = KVH * HEAD
    per_group = QH // KVH
    starts = (jnp.cumsum(row_lengths) - row_lengths).astype(jnp.int32)
    positions = jnp.arange(ROW, dtype=jnp.int32)
    segment = segment_of(starts, positions)
    picked = segment[:, None] == jnp.arange(TRAJ, dtype=jnp.int32)[None, :]
    token_weight = lax.optimization_barrier(jnp.sum(jnp.where(picked, row_advantage[None, :], 0.0), axis=1))
    weighted = (row_up.astype(jnp.float32) * token_weight[:, None]).astype(jnp.bfloat16)
    key_padded = jnp.concatenate([jnp.zeros((reach, width_kv), jnp.bfloat16), row_keys], axis=0)
    value_padded = jnp.concatenate([jnp.zeros((reach, width_kv), jnp.bfloat16), row_values], axis=0)
    seg_padded = jnp.concatenate([jnp.full((reach,), -1, jnp.int32), segment], axis=0)
    window_rows = reach + TOK_DEV

    def block_step(carry, block_index):
        key_acc, value_acc = carry
        first = (block_index * TOK_DEV).astype(jnp.int32)
        query_block = lax.dynamic_slice_in_dim(row_queries, first, TOK_DEV, 0)
        weighted_block = lax.dynamic_slice_in_dim(weighted, first, TOK_DEV, 0)
        key_block = lax.dynamic_slice_in_dim(key_padded, first, window_rows, 0)
        value_block = lax.dynamic_slice_in_dim(value_padded, first, window_rows, 0)
        seg_query = lax.dynamic_slice_in_dim(segment, first, TOK_DEV, 0)
        seg_key = lax.dynamic_slice_in_dim(seg_padded, first, window_rows, 0)
        query_pos = first + jnp.arange(TOK_DEV, dtype=jnp.int32)
        key_pos = first - reach + jnp.arange(window_rows, dtype=jnp.int32)
        allowed = (seg_key[None, :] == seg_query[:, None]) & (key_pos[None, :] <= query_pos[:, None]) & (key_pos[None, :] >= 0)
        query_split = jnp.moveaxis(query_block.reshape(TOK_DEV, KVH, per_group, HEAD), 1, 0)
        weighted_split = jnp.moveaxis(weighted_block.reshape(TOK_DEV, KVH, per_group, HEAD), 1, 0)
        key_split = jnp.moveaxis(key_block.reshape(window_rows, KVH, HEAD), 1, 0)
        value_split = jnp.moveaxis(value_block.reshape(window_rows, KVH, HEAD), 1, 0)
        query_grad, key_grad, value_grad = lax.map(lambda group_items: group_backward(group_items[0], group_items[1], group_items[2], group_items[3], allowed), (query_split, key_split, value_split, weighted_split))
        query_grad = jnp.moveaxis(query_grad, 0, 1).reshape(TOK_DEV, QH * HEAD)
        key_grad = jnp.moveaxis(key_grad, 0, 1).reshape(window_rows, width_kv)
        value_grad = jnp.moveaxis(value_grad, 0, 1).reshape(window_rows, width_kv)
        key_acc = lax.dynamic_update_slice_in_dim(key_acc, lax.dynamic_slice_in_dim(key_acc, first, window_rows, 0) + key_grad, first, 0)
        value_acc = lax.dynamic_update_slice_in_dim(value_acc, lax.dynamic_slice_in_dim(value_acc, first, window_rows, 0) + value_grad, first, 0)
        return ((key_acc, value_acc), query_grad)
    start_acc = (jnp.zeros((ROW + reach, width_kv), jnp.float32), jnp.zeros((ROW + reach, width_kv), jnp.float32))
    (key_acc, value_acc), query_blocks = lax.scan(block_step, start_acc, jnp.arange(ROW // TOK_DEV, dtype=jnp.int32))
    return (query_blocks.reshape(ROW, QH * HEAD), key_acc[reach:].astype(jnp.bfloat16), value_acc[reach:].astype(jnp.bfloat16))

def reference(queries, keys, values, upstream, lengths, group_ids, rewards):
    flat_groups = group_ids.reshape(-1)
    flat_rewards = rewards.reshape(-1)
    member = flat_groups[:, None] == jnp.arange(GROUPS, dtype=jnp.int32)[None, :]
    group_sums = lax.optimization_barrier(jnp.sum(jnp.where(member, flat_rewards[:, None], 0.0), axis=0))
    group_counts = lax.optimization_barrier(jnp.sum(member.astype(jnp.float32), axis=0))
    own_sum = lax.optimization_barrier(jnp.sum(jnp.where(member, group_sums[None, :], 0.0), axis=1))
    own_count = lax.optimization_barrier(jnp.sum(jnp.where(member, group_counts[None, :], 0.0), axis=1))
    advantage = flat_rewards - (own_sum - flat_rewards) / jnp.maximum(own_count - 1.0, 1.0)
    advantage = advantage.reshape(ROWS, TRAJ)
    query_grad, key_grad, value_grad = lax.map(lambda row_items: row_backward(row_items[0], row_items[1], row_items[2], row_items[3], row_items[4], row_items[5]), (queries, keys, values, upstream, lengths, advantage))
    return (query_grad, key_grad, value_grad)
```

```python
import math

import jax
import jax.numpy as jnp
from jax import lax
from jax.experimental import pallas as pl
from jax.experimental.pallas import tpu as pltpu
from jax.sharding import PartitionSpec as P

QH = 20
KVH = 4
HEAD = 128
SPAN = 2
GRP_ROW = 4
PER = QH // KVH
HALF = 128
ROWS = 256
REACH = 640
WINDOW = 768
SCALE = 1.0 / math.sqrt(HEAD)
EXP_SCALE = SCALE * math.log2(math.e)
EXCLUDED = -1e30


def shifted(x, axis, by):
    length = lax.axis_size(axis)
    pairs = [(i, i + by) for i in range(length) if 0 <= i + by < length]
    return lax.ppermute(x, axis, pairs)


def attention_kernel(
    low_ref, gain_ref, q_ref, u_ref, k_ref, v_ref, near_ref, far_ref,
    dq_ref, own_ref, to_near_ref, to_far_ref,
    mask, kw, vw, kt, qj, uj, s, uv, p, ds, dk, dv,
):
    f32, bf16 = jnp.float32, jnp.bfloat16

    @pl.when(pl.program_id(0) == 0)
    def _():
        for j in range(2):
            key_at = lax.broadcasted_iota(jnp.int32, (REACH, HALF), 0) + j * HALF
            query_at = lax.broadcasted_iota(jnp.int32, (REACH, HALF), 1) + (SPAN * ROWS + j * HALF)
            low = low_ref[:, j * HALF : (j + 1) * HALF]
            mask[j] = jnp.where((key_at <= query_at) & (key_at >= low), 0.0, EXCLUDED).astype(f32)

    for window, at, own in ((kw, 0, k_ref), (vw, 1, v_ref)):
        window[0:ROWS] = far_ref[at]
        window[ROWS : 2 * ROWS] = near_ref[at]
        window[2 * ROWS :] = own[...]
    kt[...] = kw[...].T
    dk[...] = jnp.zeros_like(dk)
    dv[...] = jnp.zeros_like(dv)
    for j in range(2):
        first = j * HALF
        rows = slice(first, first + HALF)
        keys = slice(first, first + REACH)
        for h in range(PER):
            cols = slice(h * HEAD, (h + 1) * HEAD)
            qj[h * HALF : (h + 1) * HALF] = q_ref[rows, cols]
            uj[h * HALF : (h + 1) * HALF] = u_ref[rows, cols]
        inner = (((1,), (1,)), ((), ()))
        s[...] = lax.dot_general(kw[keys], qj[...], inner, preferred_element_type=f32)
        uv[...] = lax.dot_general(vw[keys], uj[...], inner, preferred_element_type=f32)
        for h in range(PER):
            lanes = slice(h * HALF, (h + 1) * HALF)
            tiles = [slice(t * HALF, (t + 1) * HALF) for t in range(REACH // HALF)]
            top = None
            for tile in tiles:
                x = s[tile, lanes] + mask[j, tile]
                s[tile, lanes] = x
                part = jnp.max(x.reshape(HALF // 8, 8, HALF), axis=0)
                top = part if top is None else jnp.maximum(top, part)
            top = jnp.max(top, axis=0, keepdims=True)
            total = inner_sum = None
            for tile in tiles:
                e = jnp.exp2((s[tile, lanes] - top) * EXP_SCALE)
                s[tile, lanes] = e
                part = jnp.sum(e.reshape(HALF // 8, 8, HALF), axis=0)
                part_uv = jnp.sum((e * uv[tile, lanes]).reshape(HALF // 8, 8, HALF), axis=0)
                total = part if total is None else total + part
                inner_sum = part_uv if inner_sum is None else inner_sum + part_uv
            inverse = 1.0 / jnp.sum(total, axis=0, keepdims=True)
            delta = jnp.sum(inner_sum, axis=0, keepdims=True) * inverse
            for tile in tiles:
                soft = s[tile, lanes] * inverse
                p[tile, lanes] = soft.astype(bf16)
                ds[tile, lanes] = (soft * (uv[tile, lanes] - delta)).astype(bf16)
        dv[keys] += jnp.dot(p[...], uj[...], preferred_element_type=f32)
        dk[keys] += jnp.dot(ds[...], qj[...], preferred_element_type=f32)
        dq_t = jnp.dot(kt[:, keys], ds[...], preferred_element_type=f32)
        gain = gain_ref[:, rows]
        for h in range(PER):
            block = dq_t[:, h * HALF : (h + 1) * HALF] * gain
            dq_ref[rows, h * HEAD : (h + 1) * HEAD] = block.T.astype(bf16)
    for at, grad in ((0, dk), (1, dv)):
        to_far_ref[at] = grad[0:ROWS].astype(bf16)
        to_near_ref[at] = grad[ROWS : 2 * ROWS].astype(bf16)
        own_ref[at] = grad[2 * ROWS :]


def attention_backward(low, gain, q, u, k, v, near, far):
    f32, bf16 = jnp.float32, jnp.bfloat16
    groups = k.shape[1] // HEAD
    row = pl.BlockSpec((1, ROWS), lambda g: (0, 0))
    wide = pl.BlockSpec((ROWS, PER * HEAD), lambda g: (0, g))
    head = pl.BlockSpec((ROWS, HEAD), lambda g: (0, g))
    pair = pl.BlockSpec((2, ROWS, HEAD), lambda g: (0, 0, g))
    pair_shape = (2, ROWS, groups * HEAD)
    return pl.pallas_call(
        attention_kernel,
        grid=(groups,),
        in_specs=[row, row, wide, wide, head, head, pair, pair],
        out_specs=[wide, pair, pair, pair],
        out_shape=[
            jax.ShapeDtypeStruct(q.shape, bf16),
            jax.ShapeDtypeStruct(pair_shape, f32),
            jax.ShapeDtypeStruct(pair_shape, bf16),
            jax.ShapeDtypeStruct(pair_shape, bf16),
        ],
        scratch_shapes=[
            pltpu.VMEM((2, REACH, HALF), f32),
            pltpu.VMEM((WINDOW, HEAD), bf16),
            pltpu.VMEM((WINDOW, HEAD), bf16),
            pltpu.VMEM((HEAD, WINDOW), bf16),
            pltpu.VMEM((REACH, HEAD), bf16),
            pltpu.VMEM((REACH, HEAD), bf16),
            pltpu.VMEM((REACH, REACH), f32),
            pltpu.VMEM((REACH, REACH), f32),
            pltpu.VMEM((REACH, REACH), bf16),
            pltpu.VMEM((REACH, REACH), bf16),
            pltpu.VMEM((WINDOW, HEAD), f32),
            pltpu.VMEM((WINDOW, HEAD), f32),
        ],
        compiler_params=pltpu.CompilerParams(vmem_limit_bytes=40 * 1024 * 1024),
    )(low, gain, q, u, k, v, near, far)


def local(queries, keys, values, upstream, lengths, group_ids, rewards):
    groups_all = GRP_ROW * lax.axis_size("grp")
    pair = jnp.stack([keys[0], values[0]])
    near = shifted(pair, "ctx", 1)
    far = shifted(pair, "ctx", 2)

    row_lengths = lengths[0]
    row_rewards = rewards[0]
    member = group_ids[0][:, None] == jnp.arange(groups_all, dtype=jnp.int32)[None, :]
    local_sums = jnp.sum(jnp.where(member, row_rewards[:, None], 0.0), axis=0)
    local_counts = jnp.sum(member.astype(jnp.float32), axis=0)
    everyone = lax.all_gather(
        jnp.concatenate([local_sums, local_counts])[None], "grp", tiled=True
    )
    both = jnp.sum(everyone, axis=0)
    own_sum = jnp.sum(jnp.where(member, both[None, :groups_all], 0.0), axis=1)
    own_count = jnp.sum(jnp.where(member, both[None, groups_all:], 0.0), axis=1)
    advantage = row_rewards - (own_sum - row_rewards) / jnp.maximum(own_count - 1.0, 1.0)

    starts = jnp.cumsum(row_lengths) - row_lengths
    first_row = lax.axis_index("ctx") * ROWS
    position = first_row + jnp.arange(ROWS, dtype=jnp.int32)
    begun = starts[None, :] <= position[:, None]
    seg_start = jnp.max(jnp.where(begun, starts[None, :], 0), axis=1)
    picked = begun & (starts[None, :] == seg_start[:, None])
    token_weight = jnp.sum(jnp.where(picked, advantage[None, :], 0.0), axis=1)
    low = seg_start - (first_row - SPAN * ROWS)

    dq, own, to_near, to_far = attention_backward(
        low[None], (token_weight * SCALE)[None], queries[0], upstream[0], keys[0], values[0], near, far
    )
    total = (
        own
        + shifted(to_near, "ctx", -1).astype(jnp.float32)
        + shifted(to_far, "ctx", -2).astype(jnp.float32)
    )
    key_out = (total[0] * (token_weight * SCALE)[:, None]).astype(jnp.bfloat16)
    value_out = (total[1] * token_weight[:, None]).astype(jnp.bfloat16)
    return (dq[None], key_out[None], value_out[None])


def solution(mesh):
    in_specs = (
        P("grp", "ctx", None),
        P("grp", "ctx", None),
        P("grp", "ctx", None),
        P("grp", "ctx", None),
        P("grp", None),
        P("grp", None),
        P("grp", None),
    )
    out_specs = (P("grp", "ctx", None), P("grp", "ctx", None), P("grp", "ctx", None))
    return jax.shard_map(local, mesh=mesh, in_specs=in_specs, out_specs=out_specs, check_vma=False)
```

```python
import math

import jax
import jax.numpy as jnp
from jax import lax
from jax.experimental import pallas as pl
from jax.experimental.pallas import tpu as pltpu
from jax.sharding import PartitionSpec as P

QH = 20
KVH = 4
HEAD = 128
SPAN = 2
GRP_ROW = 4
PER = QH // KVH
HALF = 128
ROWS = 256
REACH = 640
WINDOW = 768
SCALE = 1.0 / math.sqrt(HEAD)
EXP_SCALE = SCALE * math.log2(math.e)
EXCLUDED = -1e30
PARTS = 2
VMEM_BYTES = 32 * 1024 * 1024
COST_FLOPS = 4_000_000_000


def shifted(x, axis, by):
    length = lax.axis_size(axis)
    pairs = [(i, i + by) for i in range(length) if 0 <= i + by < length]
    return lax.ppermute(x, axis, pairs)


def attention_kernel(*refs):
    low_ref, q_ref, u_ref, k_ref, v_ref, near_ref, far_ref = refs[-23:-16]
    dq_ref, own_ref, to_near_ref, to_far_ref = refs[-16:-12]
    mask, kw, vw, kt, qj, uj, s, uv, p, ds, dk, dv = refs[-12:]
    f32, bf16 = jnp.float32, jnp.bfloat16

    @pl.when(pl.program_id(0) == 0)
    def _():
        for j in range(2):
            key_at = lax.broadcasted_iota(jnp.int32, (REACH, HALF), 0) + j * HALF
            query_at = lax.broadcasted_iota(jnp.int32, (REACH, HALF), 1) + (SPAN * ROWS + j * HALF)
            low = low_ref[:, j * HALF : (j + 1) * HALF]
            mask[j] = jnp.where((key_at <= query_at) & (key_at >= low), 0.0, EXCLUDED).astype(f32)

    for window, at, own in ((kw, 0, k_ref), (vw, 1, v_ref)):
        window[0:ROWS] = far_ref[at]
        window[ROWS : 2 * ROWS] = near_ref[at]
        window[2 * ROWS :] = own[...]
    kt[...] = kw[...].T
    dk[...] = jnp.zeros_like(dk)
    dv[...] = jnp.zeros_like(dv)
    for j in range(2):
        first = j * HALF
        rows = slice(first, first + HALF)
        keys = slice(first, first + REACH)
        for h in range(PER):
            cols = slice(h * HEAD, (h + 1) * HEAD)
            qj[h * HALF : (h + 1) * HALF] = q_ref[rows, cols]
            uj[h * HALF : (h + 1) * HALF] = u_ref[rows, cols]
        inner = (((1,), (1,)), ((), ()))
        s[...] = lax.dot_general(kw[keys], qj[...], inner, preferred_element_type=f32)
        uv[...] = lax.dot_general(vw[keys], uj[...], inner, preferred_element_type=f32)
        for h in range(PER):
            lanes = slice(h * HALF, (h + 1) * HALF)
            tiles = [slice(t * HALF, (t + 1) * HALF) for t in range(REACH // HALF)]
            top = None
            for tile in tiles:
                x = s[tile, lanes] + mask[j, tile]
                s[tile, lanes] = x
                part = jnp.max(x.reshape(HALF // 8, 8, HALF), axis=0)
                top = part if top is None else jnp.maximum(top, part)
            top = jnp.max(top, axis=0, keepdims=True)
            total = inner_sum = None
            for tile in tiles:
                e = jnp.exp2((s[tile, lanes] - top) * EXP_SCALE)
                s[tile, lanes] = e
                part = jnp.sum(e.reshape(HALF // 8, 8, HALF), axis=0)
                part_uv = jnp.sum((e * uv[tile, lanes]).reshape(HALF // 8, 8, HALF), axis=0)
                total = part if total is None else total + part
                inner_sum = part_uv if inner_sum is None else inner_sum + part_uv
            inverse = 1.0 / jnp.sum(total, axis=0, keepdims=True)
            delta = jnp.sum(inner_sum, axis=0, keepdims=True) * inverse
            for tile in tiles:
                soft = s[tile, lanes] * inverse
                p[tile, lanes] = soft.astype(bf16)
                ds[tile, lanes] = (soft * (uv[tile, lanes] - delta)).astype(bf16)
        dv[keys] += jnp.dot(p[...], uj[...], preferred_element_type=f32)
        dk[keys] += jnp.dot(ds[...], qj[...], preferred_element_type=f32)
        dq_t = jnp.dot(kt[:, keys], ds[...], preferred_element_type=f32)
        for h in range(PER):
            block = dq_t[:, h * HALF : (h + 1) * HALF]
            dq_ref[rows, h * HEAD : (h + 1) * HEAD] = block.T.astype(bf16)
    for at, grad in ((0, dk), (1, dv)):
        to_far_ref[at] = grad[0:ROWS].astype(bf16)
        to_near_ref[at] = grad[ROWS : 2 * ROWS].astype(bf16)
        own_ref[at] = grad[2 * ROWS :]


def attention_backward(part, low, q, u, k, v, near, far, before):
    f32, bf16 = jnp.float32, jnp.bfloat16
    groups = far.shape[2] // HEAD
    first = part * groups
    row = pl.BlockSpec((1, ROWS), lambda g: (0, 0))
    wide = pl.BlockSpec((ROWS, PER * HEAD), lambda g: (0, first + g))
    head = pl.BlockSpec((ROWS, HEAD), lambda g: (0, first + g))
    pair = pl.BlockSpec((2, ROWS, HEAD), lambda g: (0, 0, g))
    pair_shape = (2, ROWS, groups * HEAD)
    return pl.pallas_call(
        attention_kernel,
        grid=(groups,),
        in_specs=[pl.BlockSpec(memory_space=pl.ANY)] * len(before)
        + [row, wide, wide, head, head, pair, pair],
        out_specs=[wide, pair, pair, pair],
        out_shape=[
            jax.ShapeDtypeStruct(q.shape, bf16),
            jax.ShapeDtypeStruct(pair_shape, f32),
            jax.ShapeDtypeStruct(pair_shape, bf16),
            jax.ShapeDtypeStruct(pair_shape, bf16),
        ],
        scratch_shapes=[
            pltpu.VMEM((2, REACH, HALF), f32),
            pltpu.VMEM((WINDOW, HEAD), bf16),
            pltpu.VMEM((WINDOW, HEAD), bf16),
            pltpu.VMEM((HEAD, WINDOW), bf16),
            pltpu.VMEM((REACH, HEAD), bf16),
            pltpu.VMEM((REACH, HEAD), bf16),
            pltpu.VMEM((REACH, REACH), f32),
            pltpu.VMEM((REACH, REACH), f32),
            pltpu.VMEM((REACH, REACH), bf16),
            pltpu.VMEM((REACH, REACH), bf16),
            pltpu.VMEM((WINDOW, HEAD), f32),
            pltpu.VMEM((WINDOW, HEAD), f32),
        ],
        input_output_aliases={0: 0} if before else {},
        compiler_params=pltpu.CompilerParams(vmem_limit_bytes=VMEM_BYTES),
        cost_estimate=pl.CostEstimate(
            flops=COST_FLOPS * groups,
            bytes_accessed=4 * 1024 * 1024,
            transcendentals=groups * 2 * REACH * REACH,
        ),
    )(*before, low, q, u, k, v, near, far)


def after_kernel(x_ref, *refs):
    refs[-1][...] = x_ref[...]


def after(x, *others):
    return pl.pallas_call(
        after_kernel,
        in_specs=[pl.BlockSpec(memory_space=pltpu.VMEM)] + [pl.BlockSpec(memory_space=pl.ANY)] * len(others),
        out_specs=pl.BlockSpec(memory_space=pltpu.VMEM),
        out_shape=jax.ShapeDtypeStruct(x.shape, x.dtype),
    )(x, *others)


def group_stats(group_ids, rewards):
    groups_all = GRP_ROW * lax.axis_size("grp")
    member = group_ids[:, None] == jnp.arange(groups_all, dtype=jnp.int32)[None, :]
    sums = jnp.sum(jnp.where(member, rewards[:, None], 0.0), axis=0)
    counts = jnp.sum(member.astype(jnp.float32), axis=0)
    return member, jnp.concatenate([sums, counts])[None]


def advantage_of(member, stats, rewards):
    rows, groups_all = lax.axis_size("grp"), member.shape[1]
    everyone = lax.all_to_all(
        jnp.broadcast_to(stats, (rows, stats.shape[1])), "grp", 0, 0, tiled=True
    )
    both = jnp.sum(everyone, axis=0)
    own_sum = jnp.sum(jnp.where(member, both[None, :groups_all], 0.0), axis=1)
    own_count = jnp.sum(jnp.where(member, both[None, groups_all:], 0.0), axis=1)
    return rewards - (own_sum - rewards) / jnp.maximum(own_count - 1.0, 1.0)


def local(queries, keys, values, upstream, lengths, group_ids, rewards):
    width = keys.shape[2] // PARTS
    halos = []
    for part in range(PARTS):
        cols = slice(part * width, (part + 1) * width)
        pair = jnp.stack([keys[0, :, cols], values[0, :, cols]])
        halos.append((shifted(pair, "ctx", 1), shifted(pair, "ctx", 2)))

    starts = jnp.cumsum(lengths[0]) - lengths[0]
    first_row = lax.axis_index("ctx") * ROWS
    position = first_row + jnp.arange(ROWS, dtype=jnp.int32)
    begun = starts[None, :] <= position[:, None]
    seg_start = jnp.max(jnp.where(begun, starts[None, :], 0), axis=1)
    low = (seg_start - (first_row - SPAN * ROWS))[None]

    before, received = [], []
    for part, (near, far) in enumerate(halos):
        dq, own, to_near, to_far = attention_backward(
            part, low, queries[0], upstream[0], keys[0], values[0], near, far, before
        )
        before = [dq]
        received.append((own, shifted(to_near, "ctx", -1), shifted(to_far, "ctx", -2)))

    member, stats = group_stats(group_ids[0], rewards[0])
    advantage = advantage_of(member, after(stats, *received[0][1:]), rewards[0])
    picked = begun & (starts[None, :] == seg_start[:, None])
    weight = jnp.sum(jnp.where(picked, advantage[None, :], 0.0), axis=1)[:, None]
    scaled = weight * SCALE
    dq = (dq.astype(jnp.float32) * scaled).astype(jnp.bfloat16)
    totals = [own + a.astype(jnp.float32) + b.astype(jnp.float32) for own, a, b in received]
    dk = [(t[0] * scaled).astype(jnp.bfloat16) for t in totals]
    dv = [(t[1] * weight).astype(jnp.bfloat16) for t in totals]
    return (dq[None], jnp.concatenate(dk, axis=1)[None], jnp.concatenate(dv, axis=1)[None])


def solution(mesh):
    in_specs = (
        P("grp", "ctx", None),
        P("grp", "ctx", None),
        P("grp", "ctx", None),
        P("grp", "ctx", None),
        P("grp", None),
        P("grp", None),
        P("grp", None),
    )
    out_specs = (P("grp", "ctx", None), P("grp", "ctx", None), P("grp", "ctx", None))
    return jax.shard_map(local, mesh=mesh, in_specs=in_specs, out_specs=out_specs, check_vma=False)
```

```python
import math

import jax
import jax.numpy as jnp
from jax import lax
from jax.experimental import pallas as pl
from jax.experimental.pallas import tpu as pltpu
from jax.sharding import PartitionSpec as P

QH = 20
KVH = 4
HEAD = 128
SPAN = 2
GRP_ROW = 4
PER = QH // KVH
HALF = 128
ROWS = 256
REACH = 640
WINDOW = 768
SCALE = 1.0 / math.sqrt(HEAD)
EXP_SCALE = SCALE * math.log2(math.e)
EXCLUDED = -1e30
PARTS = 2
VMEM_BYTES = 32 * 1024 * 1024
COST_FLOPS = 4_000_000_000


def shifted(x, axis, by):
    length = lax.axis_size(axis)
    pairs = [(i, i + by) for i in range(length) if 0 <= i + by < length]
    return lax.ppermute(x, axis, pairs)


def attention_kernel(*refs):
    far_ref, near_ref, low_ref, q_ref, u_ref, k_ref, v_ref = refs[-23:-16]
    dq_ref, own_ref, to_near_ref, to_far_ref = refs[-16:-12]
    mask, kw, vw, kt, qj, uj, s, uv, p, ds, dk, dv = refs[-12:]
    f32, bf16 = jnp.float32, jnp.bfloat16

    @pl.when(pl.program_id(0) == 0)
    def _():
        for j in range(2):
            key_at = lax.broadcasted_iota(jnp.int32, (REACH, HALF), 0) + j * HALF
            query_at = lax.broadcasted_iota(jnp.int32, (REACH, HALF), 1) + (SPAN * ROWS + j * HALF)
            low = low_ref[:, j * HALF : (j + 1) * HALF]
            mask[j] = jnp.where((key_at <= query_at) & (key_at >= low), 0.0, EXCLUDED).astype(f32)

    for window, at, own in ((kw, 0, k_ref), (vw, 1, v_ref)):
        window[0:ROWS] = far_ref[at]
        window[ROWS : 2 * ROWS] = near_ref[at]
        window[2 * ROWS :] = own[...]
    kt[...] = kw[...].T
    dk[...] = jnp.zeros_like(dk)
    dv[...] = jnp.zeros_like(dv)
    for j in range(2):
        first = j * HALF
        rows = slice(first, first + HALF)
        keys = slice(first, first + REACH)
        for h in range(PER):
            cols = slice(h * HEAD, (h + 1) * HEAD)
            qj[h * HALF : (h + 1) * HALF] = q_ref[rows, cols]
            uj[h * HALF : (h + 1) * HALF] = u_ref[rows, cols]
        inner = (((1,), (1,)), ((), ()))
        s[...] = lax.dot_general(kw[keys], qj[...], inner, preferred_element_type=f32)
        uv[...] = lax.dot_general(vw[keys], uj[...], inner, preferred_element_type=f32)
        for h in range(PER):
            lanes = slice(h * HALF, (h + 1) * HALF)
            tiles = [slice(t * HALF, (t + 1) * HALF) for t in range(REACH // HALF)]
            top = None
            for tile in tiles:
                x = s[tile, lanes] + mask[j, tile]
                s[tile, lanes] = x
                part = jnp.max(x.reshape(HALF // 8, 8, HALF), axis=0)
                top = part if top is None else jnp.maximum(top, part)
            top = jnp.max(top, axis=0, keepdims=True)
            total = inner_sum = None
            for tile in tiles:
                e = jnp.exp2((s[tile, lanes] - top) * EXP_SCALE)
                s[tile, lanes] = e
                part = jnp.sum(e.reshape(HALF // 8, 8, HALF), axis=0)
                part_uv = jnp.sum((e * uv[tile, lanes]).reshape(HALF // 8, 8, HALF), axis=0)
                total = part if total is None else total + part
                inner_sum = part_uv if inner_sum is None else inner_sum + part_uv
            inverse = 1.0 / jnp.sum(total, axis=0, keepdims=True)
            delta = jnp.sum(inner_sum, axis=0, keepdims=True) * inverse
            for tile in tiles:
                soft = s[tile, lanes] * inverse
                p[tile, lanes] = soft.astype(bf16)
                ds[tile, lanes] = (soft * (uv[tile, lanes] - delta)).astype(bf16)
        dv[keys] += jnp.dot(p[...], uj[...], preferred_element_type=f32)
        dk[keys] += jnp.dot(ds[...], qj[...], preferred_element_type=f32)
        dq_t = jnp.dot(kt[:, keys], ds[...], preferred_element_type=f32)
        for h in range(PER):
            block = dq_t[:, h * HALF : (h + 1) * HALF]
            dq_ref[rows, h * HEAD : (h + 1) * HEAD] = block.T.astype(bf16)
    for at, grad in ((0, dk), (1, dv)):
        to_far_ref[at] = grad[0:ROWS].astype(bf16)
        to_near_ref[at] = grad[ROWS : 2 * ROWS].astype(bf16)
        own_ref[at] = grad[2 * ROWS :]


def attention_backward(part, low, q, u, k, v, near, far, before):
    f32, bf16 = jnp.float32, jnp.bfloat16
    groups = far.shape[2] // HEAD
    q, u = (pltpu.with_memory_space_constraint(x, pltpu.HBM) for x in (q, u))
    first = part * groups
    row = pl.BlockSpec((1, ROWS), lambda g: (0, 0))
    wide = pl.BlockSpec((ROWS, PER * HEAD), lambda g: (0, first + g))
    head = pl.BlockSpec((ROWS, HEAD), lambda g: (0, first + g))
    pair = pl.BlockSpec((2, ROWS, HEAD), lambda g: (0, 0, g))
    pair_shape = (2, ROWS, groups * HEAD)
    return pl.pallas_call(
        attention_kernel,
        grid=(groups,),
        in_specs=[pl.BlockSpec(memory_space=pl.ANY)] * len(before)
        + [pair, pair, row, wide, wide, head, head],
        out_specs=[wide, pair, pair, pair],
        out_shape=[
            jax.ShapeDtypeStruct(q.shape, bf16),
            jax.ShapeDtypeStruct(pair_shape, f32),
            jax.ShapeDtypeStruct(pair_shape, bf16),
            jax.ShapeDtypeStruct(pair_shape, bf16),
        ],
        scratch_shapes=[
            pltpu.VMEM((2, REACH, HALF), f32),
            pltpu.VMEM((WINDOW, HEAD), bf16),
            pltpu.VMEM((WINDOW, HEAD), bf16),
            pltpu.VMEM((HEAD, WINDOW), bf16),
            pltpu.VMEM((REACH, HEAD), bf16),
            pltpu.VMEM((REACH, HEAD), bf16),
            pltpu.VMEM((REACH, REACH), f32),
            pltpu.VMEM((REACH, REACH), f32),
            pltpu.VMEM((REACH, REACH), bf16),
            pltpu.VMEM((REACH, REACH), bf16),
            pltpu.VMEM((WINDOW, HEAD), f32),
            pltpu.VMEM((WINDOW, HEAD), f32),
        ],
        input_output_aliases={0: 0} if before else {},
        compiler_params=pltpu.CompilerParams(vmem_limit_bytes=VMEM_BYTES),
        cost_estimate=pl.CostEstimate(
            flops=COST_FLOPS * groups,
            bytes_accessed=4 * 1024 * 1024,
            transcendentals=groups * 2 * REACH * REACH,
        ),
    )(*before, far, near, low, q, u, k, v)


def stats_kernel(ids_ref, rewards_ref, _, out_ref):
    copies, groups_all = out_ref.shape[0], out_ref.shape[2] // 2
    ids = jnp.broadcast_to(ids_ref[...], (groups_all, ids_ref.shape[1]))
    member = (ids == lax.broadcasted_iota(jnp.int32, ids.shape, 0)).astype(jnp.float32)
    rewards = jnp.broadcast_to(rewards_ref[...], (copies, ids.shape[1]))
    sums, counts = (
        lax.dot_general(
            x, member, (((1,), (1,)), ((), ())),
            precision=lax.Precision.HIGHEST, preferred_element_type=jnp.float32,
        )
        for x in (rewards, jnp.ones_like(rewards))
    )
    stats = jnp.concatenate([sums, counts], axis=1)
    for i in range(copies):
        out_ref[i] = stats[i : i + 1]


def stats_after(group_ids, rewards, copies, other):
    vmem = pl.BlockSpec(memory_space=pltpu.VMEM)
    return pl.pallas_call(
        stats_kernel,
        in_specs=[vmem, vmem, pl.BlockSpec(memory_space=pl.ANY)],
        out_specs=vmem,
        out_shape=jax.ShapeDtypeStruct((copies, 1, 2 * GRP_ROW * copies), rewards.dtype),
    )(group_ids, rewards, other)


def advantage_of(group_ids, rewards, stats):
    both = jnp.sum(lax.all_to_all(stats, "grp", 0, 0, tiled=True), axis=(0, 1))[None]
    groups_all = both.shape[1] // 2
    member = group_ids[:, None] == jnp.arange(groups_all, dtype=jnp.int32)[None, :]
    own_sum = jnp.sum(jnp.where(member, both[:, :groups_all], 0.0), axis=1)
    own_count = jnp.sum(jnp.where(member, both[:, groups_all:], 0.0), axis=1)
    return rewards - (own_sum - rewards) / jnp.maximum(own_count - 1.0, 1.0)


def local(queries, keys, values, upstream, lengths, group_ids, rewards):
    width = keys.shape[2] // PARTS
    halos = []
    for part in range(PARTS):
        cols = slice(part * width, (part + 1) * width)
        pair = jnp.stack([keys[0, :, cols], values[0, :, cols]])
        halos.append((shifted(pair, "ctx", 1), shifted(pair, "ctx", 2)))

    starts = jnp.cumsum(lengths[0]) - lengths[0]
    first_row = lax.axis_index("ctx") * ROWS
    position = first_row + jnp.arange(ROWS, dtype=jnp.int32)
    begun = starts[None, :] <= position[:, None]
    seg_start = jnp.max(jnp.where(begun, starts[None, :], 0), axis=1)
    low = (seg_start - (first_row - SPAN * ROWS))[None]

    before, received = [], []
    for part, (near, far) in enumerate(halos):
        dq, own, to_near, to_far = attention_backward(
            part, low, queries[0], upstream[0], keys[0], values[0], near, far, before
        )
        before = [dq]
        received.append((own, shifted(to_near, "ctx", -1), shifted(to_far, "ctx", -2)))

    stats = stats_after(group_ids, rewards, lax.axis_size("grp"), received[0][2])
    advantage = advantage_of(group_ids[0], rewards[0], stats)
    picked = begun & (starts[None, :] == seg_start[:, None])
    weight = jnp.sum(jnp.where(picked, advantage[None, :], 0.0), axis=1)[:, None]
    scaled = weight * SCALE
    dq = (dq.astype(jnp.float32) * scaled).astype(jnp.bfloat16)
    totals = [own + a.astype(jnp.float32) + b.astype(jnp.float32) for own, a, b in received]
    dk = [(t[0] * scaled).astype(jnp.bfloat16) for t in totals]
    dv = [(t[1] * weight).astype(jnp.bfloat16) for t in totals]
    return (dq[None], jnp.concatenate(dk, axis=1)[None], jnp.concatenate(dv, axis=1)[None])


def solution(mesh):
    in_specs = (
        P("grp", "ctx", None),
        P("grp", "ctx", None),
        P("grp", "ctx", None),
        P("grp", "ctx", None),
        P("grp", None),
        P("grp", None),
        P("grp", None),
    )
    out_specs = (P("grp", "ctx", None), P("grp", "ctx", None), P("grp", "ctx", None))
    return jax.shard_map(local, mesh=mesh, in_specs=in_specs, out_specs=out_specs, check_vma=False)
```

```python
import functools
import math

import jax
import jax.numpy as jnp
from jax import lax
from jax.experimental import pallas as pl
from jax.experimental.pallas import tpu as pltpu
from jax.sharding import PartitionSpec as P

QH = 20
KVH = 4
HEAD = 128
SPAN = 2
GRP_ROW = 4
PER = QH // KVH
HALF = 128
ROWS = 256
REACH = 640
WINDOW = 768
SCALE = 1.0 / math.sqrt(HEAD)
EXP_SCALE = SCALE * math.log2(math.e)
EXCLUDED = -1e30
PARTS = 2
VMEM_BYTES = 24 * 1024 * 1024
COST_FLOPS = 4_000_000_000


def shifted(x, axis, by):
    length = lax.axis_size(axis)
    pairs = [(i, i + by) for i in range(length) if 0 <= i + by < length]
    return lax.ppermute(x, axis, pairs)


def attention_kernel(ahead, *refs):
    if ahead:
        for source, target in zip(refs[-20:-18], refs[-14:-12], strict=True):
            target[...] = source[...]
        refs = refs[:-20] + refs[-18:-14] + refs[-12:]
    far_ref, near_ref, low_ref, q_ref, u_ref, k_ref, v_ref = refs[-23:-16]
    dq_ref, own_ref, to_near_ref, to_far_ref = refs[-16:-12]
    mask, kw, vw, kt, qj, uj, s, uv, p, ds, dk, dv = refs[-12:]
    f32, bf16 = jnp.float32, jnp.bfloat16

    @pl.when(pl.program_id(0) == 0)
    def _():
        for j in range(2):
            key_at = lax.broadcasted_iota(jnp.int32, (REACH, HALF), 0) + j * HALF
            query_at = lax.broadcasted_iota(jnp.int32, (REACH, HALF), 1) + (SPAN * ROWS + j * HALF)
            low = low_ref[:, j * HALF : (j + 1) * HALF]
            mask[j] = jnp.where((key_at <= query_at) & (key_at >= low), 0.0, EXCLUDED).astype(f32)

    for window, at, own in ((kw, 0, k_ref), (vw, 1, v_ref)):
        window[0:ROWS] = far_ref[at]
        window[ROWS : 2 * ROWS] = near_ref[at]
        window[2 * ROWS :] = own[...]
    kt[...] = kw[...].T
    for j in range(2):
        first = j * HALF
        rows = slice(first, first + HALF)
        keys = slice(first, first + REACH)
        for h in range(PER):
            cols = slice(h * HEAD, (h + 1) * HEAD)
            qj[h * HALF : (h + 1) * HALF] = q_ref[rows, cols]
            uj[h * HALF : (h + 1) * HALF] = u_ref[rows, cols]
        inner = (((1,), (1,)), ((), ()))
        s[...] = lax.dot_general(kw[keys], qj[...], inner, preferred_element_type=f32)
        uv[...] = lax.dot_general(vw[keys], uj[...], inner, preferred_element_type=f32)
        for h in range(PER):
            lanes = slice(h * HALF, (h + 1) * HALF)
            tiles = [slice(t * HALF, (t + 1) * HALF) for t in range(REACH // HALF)]
            top = None
            for tile in tiles:
                x = s[tile, lanes] + mask[j, tile]
                s[tile, lanes] = x
                part = jnp.max(x.reshape(HALF // 8, 8, HALF), axis=0)
                top = part if top is None else jnp.maximum(top, part)
            top = jnp.max(top, axis=0, keepdims=True)
            total = inner_sum = None
            for tile in tiles:
                e = jnp.exp2((s[tile, lanes] - top) * EXP_SCALE)
                s[tile, lanes] = e
                part = jnp.sum(e.reshape(HALF // 8, 8, HALF), axis=0)
                part_uv = jnp.sum((e * uv[tile, lanes]).reshape(HALF // 8, 8, HALF), axis=0)
                total = part if total is None else total + part
                inner_sum = part_uv if inner_sum is None else inner_sum + part_uv
            inverse = 1.0 / jnp.sum(total, axis=0, keepdims=True)
            delta = jnp.sum(inner_sum, axis=0, keepdims=True) * inverse
            for tile in tiles:
                soft = s[tile, lanes] * inverse
                p[tile, lanes] = soft.astype(bf16)
                ds[tile, lanes] = (soft * (uv[tile, lanes] - delta)).astype(bf16)
        for grad, left, right in ((dv, p, uj), (dk, ds, qj)):
            part = jnp.dot(left[...], right[...], preferred_element_type=f32)
            if j == 0:
                grad[:REACH] = part
            else:
                grad[HALF:REACH] += part[: REACH - HALF]
                grad[REACH:] = part[REACH - HALF :]
        dq_t = jnp.dot(kt[:, keys], ds[...], preferred_element_type=f32)
        for h in range(PER):
            block = dq_t[:, h * HALF : (h + 1) * HALF]
            dq_ref[rows, h * HEAD : (h + 1) * HEAD] = block.T.astype(bf16)
    for at, grad in ((0, dk), (1, dv)):
        to_far_ref[at] = grad[0:ROWS].astype(bf16)
        to_near_ref[at] = grad[ROWS : 2 * ROWS].astype(bf16)
        own_ref[at] = grad[2 * ROWS :]


def attention_backward(part, low, q, u, taken, k, v, near, far, before):
    f32, bf16 = jnp.float32, jnp.bfloat16
    groups = far.shape[2] // HEAD
    first, after = part * groups, (part + 1) * groups
    hbm = [pltpu.with_memory_space_constraint(x, pltpu.HBM) for x in (q, u)]
    ahead = 2 * (part < PARTS - 1)
    row = pl.BlockSpec((1, ROWS), lambda g: (0, 0))
    wide = pl.BlockSpec((ROWS, PER * HEAD), lambda g: (0, first + g))
    wide_part = pl.BlockSpec((ROWS, PER * HEAD), lambda g: (0, g))
    wide_next = pl.BlockSpec((ROWS, PER * HEAD), lambda g: (0, after + g))
    head = pl.BlockSpec((ROWS, HEAD), lambda g: (0, first + g))
    pair = pl.BlockSpec((2, ROWS, HEAD), lambda g: (0, 0, g))
    pair_shape = (2, ROWS, groups * HEAD)
    part_shape = jax.ShapeDtypeStruct((ROWS, groups * PER * HEAD), bf16)
    return pl.pallas_call(
        functools.partial(attention_kernel, ahead),
        grid=(groups,),
        in_specs=[pl.BlockSpec(memory_space=pl.ANY)] * len(before)
        + [pair, pair, row]
        + [wide_part if taken else wide] * 2
        + [head, head]
        + [wide_next] * ahead,
        out_specs=[wide, pair, pair, pair] + [wide_part] * ahead,
        out_shape=[
            jax.ShapeDtypeStruct(q.shape, bf16),
            jax.ShapeDtypeStruct(pair_shape, f32),
            jax.ShapeDtypeStruct(pair_shape, bf16),
            jax.ShapeDtypeStruct(pair_shape, bf16),
        ]
        + [part_shape] * ahead,
        scratch_shapes=[
            pltpu.VMEM((2, REACH, HALF), f32),
            pltpu.VMEM((WINDOW, HEAD), bf16),
            pltpu.VMEM((WINDOW, HEAD), bf16),
            pltpu.VMEM((HEAD, WINDOW), bf16),
            pltpu.VMEM((REACH, HEAD), bf16),
            pltpu.VMEM((REACH, HEAD), bf16),
            pltpu.VMEM((REACH, REACH), f32),
            pltpu.VMEM((REACH, REACH), f32),
            pltpu.VMEM((REACH, REACH), bf16),
            pltpu.VMEM((REACH, REACH), bf16),
            pltpu.VMEM((WINDOW, HEAD), f32),
            pltpu.VMEM((WINDOW, HEAD), f32),
        ],
        input_output_aliases={0: 0} if before else {},
        compiler_params=pltpu.CompilerParams(vmem_limit_bytes=VMEM_BYTES),
        cost_estimate=pl.CostEstimate(
            flops=COST_FLOPS * groups,
            bytes_accessed=4 * 1024 * 1024,
            transcendentals=groups * 2 * REACH * REACH,
        ),
    )(*before, far, near, low, *(taken or hbm), k, v, *hbm[:ahead])


def stats_kernel(ids_ref, rewards_ref, _, out_ref):
    copies, groups_all = out_ref.shape[0], out_ref.shape[2] // 2
    ids = jnp.broadcast_to(ids_ref[...], (groups_all, ids_ref.shape[1]))
    member = (ids == lax.broadcasted_iota(jnp.int32, ids.shape, 0)).astype(jnp.float32)
    rewards = jnp.broadcast_to(rewards_ref[...], (copies, ids.shape[1]))
    sums, counts = (
        lax.dot_general(
            x, member, (((1,), (1,)), ((), ())),
            precision=lax.Precision.HIGHEST, preferred_element_type=jnp.float32,
        )
        for x in (rewards, jnp.ones_like(rewards))
    )
    stats = jnp.concatenate([sums, counts], axis=1)
    for i in range(copies):
        out_ref[i] = stats[i : i + 1]


def stats_after(group_ids, rewards, copies, other):
    vmem = pl.BlockSpec(memory_space=pltpu.VMEM)
    return pl.pallas_call(
        stats_kernel,
        in_specs=[vmem, vmem, pl.BlockSpec(memory_space=pl.ANY)],
        out_specs=vmem,
        out_shape=jax.ShapeDtypeStruct((copies, 1, 2 * GRP_ROW * copies), rewards.dtype),
    )(group_ids, rewards, other)


def advantage_of(group_ids, rewards, stats):
    both = jnp.sum(lax.all_to_all(stats, "grp", 0, 0, tiled=True), axis=(0, 1))[None]
    groups_all = both.shape[1] // 2
    member = group_ids[:, None] == jnp.arange(groups_all, dtype=jnp.int32)[None, :]
    own_sum = jnp.sum(jnp.where(member, both[:, :groups_all], 0.0), axis=1)
    own_count = jnp.sum(jnp.where(member, both[:, groups_all:], 0.0), axis=1)
    return rewards - (own_sum - rewards) / jnp.maximum(own_count - 1.0, 1.0)


def local(queries, keys, values, upstream, lengths, group_ids, rewards):
    width = keys.shape[2] // PARTS
    halos = []
    for part in range(PARTS):
        cols = slice(part * width, (part + 1) * width)
        pair = jnp.stack([keys[0, :, cols], values[0, :, cols]])
        halos.append((shifted(pair, "ctx", 1), shifted(pair, "ctx", 2)))

    starts = jnp.cumsum(lengths[0]) - lengths[0]
    first_row = lax.axis_index("ctx") * ROWS
    position = first_row + jnp.arange(ROWS, dtype=jnp.int32)
    begun = starts[None, :] <= position[:, None]
    seg_start = jnp.max(jnp.where(begun, starts[None, :], 0), axis=1)
    low = (seg_start - (first_row - SPAN * ROWS))[None]

    before, taken, received = [], [], []
    for part, (near, far) in enumerate(halos):
        dq, own, to_near, to_far, *taken = attention_backward(
            part, low, queries[0], upstream[0], taken, keys[0], values[0], near, far, before
        )
        before = [dq]
        received.append((own, shifted(to_far, "ctx", -2), shifted(to_near, "ctx", -1)))

    stats = stats_after(group_ids, rewards, lax.axis_size("grp"), received[0][1])
    advantage = advantage_of(group_ids[0], rewards[0], stats)
    picked = begun & (starts[None, :] == seg_start[:, None])
    weight = jnp.sum(jnp.where(picked, advantage[None, :], 0.0), axis=1)[:, None]
    scaled = weight * SCALE
    dq = (dq.astype(jnp.float32) * scaled).astype(jnp.bfloat16)
    total = jnp.concatenate(
        [own + a.astype(jnp.float32) + b.astype(jnp.float32) for own, a, b in received], axis=2
    )
    dk = (total[0] * scaled).astype(jnp.bfloat16)
    dv = (total[1] * weight).astype(jnp.bfloat16)
    return (dq[None], dk[None], dv[None])


def solution(mesh):
    in_specs = (
        P("grp", "ctx", None),
        P("grp", "ctx", None),
        P("grp", "ctx", None),
        P("grp", "ctx", None),
        P("grp", None),
        P("grp", None),
        P("grp", None),
    )
    out_specs = (P("grp", "ctx", None), P("grp", "ctx", None), P("grp", "ctx", None))
    return jax.shard_map(local, mesh=mesh, in_specs=in_specs, out_specs=out_specs, check_vma=False)
```

```python
import functools
import math

import jax
import jax.numpy as jnp
from jax import lax
from jax.experimental import pallas as pl
from jax.experimental.pallas import tpu as pltpu
from jax.sharding import PartitionSpec as P

QH = 20
KVH = 4
HEAD = 128
SPAN = 2
GRP_ROW = 4
PER = QH // KVH
HALF = 128
ROWS = 256
REACH = 640
WINDOW = 768
SCALE = 1.0 / math.sqrt(HEAD)
EXP_SCALE = SCALE * math.log2(math.e)
EXCLUDED = -1e30
PARTS = 2
VMEM_BYTES = 24 * 1024 * 1024
COST_FLOPS = 4_000_000_000


def shifted(x, axis, by):
    length = lax.axis_size(axis)
    pairs = [(i, i + by) for i in range(length) if 0 <= i + by < length]
    return lax.ppermute(x, axis, pairs)


def attention_kernel(ahead, *refs):
    if ahead:
        for source, target in zip(refs[-20:-18], refs[-14:-12], strict=True):
            target[...] = source[...]
        refs = refs[:-20] + refs[-18:-14] + refs[-12:]
    far_ref, near_ref, low_ref, q_ref, u_ref, k_ref, v_ref = refs[-23:-16]
    dq_ref, own_ref, to_near_ref, to_far_ref = refs[-16:-12]
    mask, kw, vw, kt, qj, uj, s, uv, p, ds, dk, dv = refs[-12:]
    f32, bf16 = jnp.float32, jnp.bfloat16

    @pl.when(pl.program_id(0) == 0)
    def _():
        for j in range(2):
            key_at = lax.broadcasted_iota(jnp.int32, (REACH, HALF), 0) + j * HALF
            query_at = lax.broadcasted_iota(jnp.int32, (REACH, HALF), 1) + (SPAN * ROWS + j * HALF)
            low = low_ref[:, j * HALF : (j + 1) * HALF]
            mask[j] = jnp.where((key_at <= query_at) & (key_at >= low), 0.0, EXCLUDED).astype(f32)

    for window, at, own in ((kw, 0, k_ref), (vw, 1, v_ref)):
        window[0:ROWS] = far_ref[at]
        window[ROWS : 2 * ROWS] = near_ref[at]
        window[2 * ROWS :] = own[...]
    kt[...] = kw[...].T
    for j in range(2):
        first = j * HALF
        rows = slice(first, first + HALF)
        keys = slice(first, first + REACH)
        for h in range(PER):
            cols = slice(h * HEAD, (h + 1) * HEAD)
            qj[h * HALF : (h + 1) * HALF] = q_ref[rows, cols]
            uj[h * HALF : (h + 1) * HALF] = u_ref[rows, cols]
        inner = (((1,), (1,)), ((), ()))
        s[...] = lax.dot_general(kw[keys], qj[...], inner, preferred_element_type=f32)
        uv[...] = lax.dot_general(vw[keys], uj[...], inner, preferred_element_type=f32)
        for h in range(PER):
            lanes = slice(h * HALF, (h + 1) * HALF)
            tiles = [slice(t * HALF, (t + 1) * HALF) for t in range(REACH // HALF)]
            top = None
            for tile in tiles:
                x = s[tile, lanes] + mask[j, tile]
                s[tile, lanes] = x
                part = jnp.max(x.reshape(HALF // 8, 8, HALF), axis=0)
                top = part if top is None else jnp.maximum(top, part)
            top = jnp.max(top, axis=0, keepdims=True)
            total = inner_sum = None
            for tile in tiles:
                e = jnp.exp2((s[tile, lanes] - top) * EXP_SCALE)
                s[tile, lanes] = e
                part = jnp.sum(e.reshape(HALF // 8, 8, HALF), axis=0)
                part_uv = jnp.sum((e * uv[tile, lanes]).reshape(HALF // 8, 8, HALF), axis=0)
                total = part if total is None else total + part
                inner_sum = part_uv if inner_sum is None else inner_sum + part_uv
            inverse = 1.0 / jnp.sum(total, axis=0, keepdims=True)
            delta = jnp.sum(inner_sum, axis=0, keepdims=True) * inverse
            for tile in tiles:
                soft = s[tile, lanes] * inverse
                p[tile, lanes] = soft.astype(bf16)
                ds[tile, lanes] = (soft * (uv[tile, lanes] - delta)).astype(bf16)
        for grad, left, right in ((dv, p, uj), (dk, ds, qj)):
            part = jnp.dot(left[...], right[...], preferred_element_type=f32)
            if j == 0:
                grad[:REACH] = part
            else:
                grad[HALF:REACH] += part[: REACH - HALF]
                grad[REACH:] = part[REACH - HALF :]
        dq_t = jnp.dot(kt[:, keys], ds[...], preferred_element_type=f32)
        for h in range(PER):
            block = dq_t[:, h * HALF : (h + 1) * HALF]
            dq_ref[rows, h * HEAD : (h + 1) * HEAD] = block.T.astype(bf16)
    for at, grad in ((0, dk), (1, dv)):
        to_far_ref[at] = grad[0:ROWS].astype(bf16)
        to_near_ref[at] = grad[ROWS : 2 * ROWS].astype(bf16)
        own_ref[at] = grad[2 * ROWS :]


def attention_backward(part, low, q, u, taken, k, v, near, far, before):
    f32, bf16 = jnp.float32, jnp.bfloat16
    groups = far.shape[2] // HEAD
    first, after = part * groups, (part + 1) * groups
    hbm = [pltpu.with_memory_space_constraint(x, pltpu.HBM) for x in (q, u)]
    ahead = 2 * (part < PARTS - 1)
    row = pl.BlockSpec((1, ROWS), lambda g: (0, 0))
    wide = pl.BlockSpec((ROWS, PER * HEAD), lambda g: (0, first + g))
    wide_part = pl.BlockSpec((ROWS, PER * HEAD), lambda g: (0, g))
    wide_next = pl.BlockSpec((ROWS, PER * HEAD), lambda g: (0, after + g))
    head = pl.BlockSpec((ROWS, HEAD), lambda g: (0, first + g))
    pair = pl.BlockSpec((2, ROWS, HEAD), lambda g: (0, 0, g))
    pair_shape = (2, ROWS, groups * HEAD)
    part_shape = jax.ShapeDtypeStruct((ROWS, groups * PER * HEAD), bf16)
    return pl.pallas_call(
        functools.partial(attention_kernel, ahead),
        grid=(groups,),
        in_specs=[pl.BlockSpec(memory_space=pl.ANY)] * len(before)
        + [pair, pair, row]
        + [wide_part if taken else wide] * 2
        + [head, head]
        + [wide_next] * ahead,
        out_specs=[wide, pair, pair, pair] + [wide_part] * ahead,
        out_shape=[
            jax.ShapeDtypeStruct(q.shape, bf16),
            jax.ShapeDtypeStruct(pair_shape, f32),
            jax.ShapeDtypeStruct(pair_shape, bf16),
            jax.ShapeDtypeStruct(pair_shape, bf16),
        ]
        + [part_shape] * ahead,
        scratch_shapes=[
            pltpu.VMEM((2, REACH, HALF), f32),
            pltpu.VMEM((WINDOW, HEAD), bf16),
            pltpu.VMEM((WINDOW, HEAD), bf16),
            pltpu.VMEM((HEAD, WINDOW), bf16),
            pltpu.VMEM((REACH, HEAD), bf16),
            pltpu.VMEM((REACH, HEAD), bf16),
            pltpu.VMEM((REACH, REACH), f32),
            pltpu.VMEM((REACH, REACH), f32),
            pltpu.VMEM((REACH, REACH), bf16),
            pltpu.VMEM((REACH, REACH), bf16),
            pltpu.VMEM((WINDOW, HEAD), f32),
            pltpu.VMEM((WINDOW, HEAD), f32),
        ],
        input_output_aliases={0: 0} if before else {},
        compiler_params=pltpu.CompilerParams(vmem_limit_bytes=VMEM_BYTES),
        cost_estimate=pl.CostEstimate(
            flops=COST_FLOPS * groups,
            bytes_accessed=4 * 1024 * 1024,
            transcendentals=groups * 2 * REACH * REACH,
        ),
    )(*before, far, near, low, *(taken or hbm), k, v, *hbm[:ahead])


def spread_kernel(x_ref, _, out_ref):
    out_ref[...] = jnp.broadcast_to(x_ref[...][None], out_ref.shape)


def stats_after(group_ids, rewards, copies, other):
    member = group_ids[0][:, None] == jnp.arange(GRP_ROW * copies, dtype=jnp.int32)[None, :]
    sums = jnp.sum(jnp.where(member, rewards[0][:, None], 0.0), axis=0)
    counts = jnp.sum(member.astype(jnp.float32), axis=0)
    stats = jnp.concatenate([sums, counts])[None]
    vmem = pl.BlockSpec(memory_space=pltpu.VMEM)
    return pl.pallas_call(
        spread_kernel,
        in_specs=[vmem, pl.BlockSpec(memory_space=pl.ANY)],
        out_specs=vmem,
        out_shape=jax.ShapeDtypeStruct((copies, *stats.shape), stats.dtype),
    )(stats, other)


def advantage_of(group_ids, rewards, stats):
    both = jnp.sum(lax.all_to_all(stats, "grp", 0, 0, tiled=True), axis=(0, 1))[None]
    groups_all = both.shape[1] // 2
    member = group_ids[:, None] == jnp.arange(groups_all, dtype=jnp.int32)[None, :]
    own_sum = jnp.sum(jnp.where(member, both[:, :groups_all], 0.0), axis=1)
    own_count = jnp.sum(jnp.where(member, both[:, groups_all:], 0.0), axis=1)
    return rewards - (own_sum - rewards) / jnp.maximum(own_count - 1.0, 1.0)


def local(queries, keys, values, upstream, lengths, group_ids, rewards):
    width = keys.shape[2] // PARTS
    halos = []
    for part in range(PARTS):
        cols = slice(part * width, (part + 1) * width)
        pair = jnp.stack([keys[0, :, cols], values[0, :, cols]])
        halos.append((shifted(pair, "ctx", 1), shifted(pair, "ctx", 2)))

    index = jnp.arange(lengths.shape[1], dtype=jnp.int32)
    starts = jnp.sum(jnp.where(index[None, :] < index[:, None], lengths, 0), axis=1)
    first_row = lax.axis_index("ctx") * ROWS
    position = first_row + jnp.arange(ROWS, dtype=jnp.int32)
    begun = starts[None, :] <= position[:, None]
    seg_start = jnp.max(jnp.where(begun, starts[None, :], 0), axis=1)
    low = (seg_start - (first_row - SPAN * ROWS))[None]

    before, taken, received = [], [], []
    for part, (near, far) in enumerate(halos):
        dq, own, to_near, to_far, *taken = attention_backward(
            part, low, queries[0], upstream[0], taken, keys[0], values[0], near, far, before
        )
        before = [dq]
        received.append((own, shifted(to_far, "ctx", -2), shifted(to_near, "ctx", -1)))

    stats = stats_after(group_ids, rewards, lax.axis_size("grp"), received[0][1])
    advantage = advantage_of(group_ids[0], rewards[0], stats)
    picked = begun & (starts[None, :] == seg_start[:, None])
    weight = jnp.sum(jnp.where(picked, advantage[None, :], 0.0), axis=1)[:, None]
    scaled = weight * SCALE
    dq = (dq.astype(jnp.float32) * scaled).astype(jnp.bfloat16)
    total = jnp.concatenate(
        [own + a.astype(jnp.float32) + b.astype(jnp.float32) for own, a, b in received], axis=2
    )
    dk = (total[0] * scaled).astype(jnp.bfloat16)
    dv = (total[1] * weight).astype(jnp.bfloat16)
    return (dq[None], dk[None], dv[None])


def solution(mesh):
    in_specs = (
        P("grp", "ctx", None),
        P("grp", "ctx", None),
        P("grp", "ctx", None),
        P("grp", "ctx", None),
        P("grp", None),
        P("grp", None),
        P("grp", None),
    )
    out_specs = (P("grp", "ctx", None), P("grp", "ctx", None), P("grp", "ctx", None))
    return jax.shard_map(local, mesh=mesh, in_specs=in_specs, out_specs=out_specs, check_vma=False)
```
